1024 devices in a mesh: replica: 32 (over x, y, core), mp: 32 (over z).
Axes of the slice: x: 4, y: 4, z: 32, core: 2. Of those that a mesh axis runs over, the one named last changes fastest.
Arguments:
- table: float32 [65536, 128], P('mp'), may hold values from -3 to 3
- accum: float32 [65536, 128], P('mp'), may hold values from 0.01 to 4
- request_ids: int32 [1024, 32, 128], P(('replica', 'mp')), may hold values from 0 to 2047
- send_counts: int32 [1024, 32], P(('replica', 'mp')), may hold values from 1 to 128, as said below
- entry_slots: int32 [262144, 16], P(('replica', 'mp')), may hold values from 0 to 4095
- entry_weights: bfloat16 [262144, 16], P(('replica', 'mp')), may hold values from 0.25 to 2
- pooled_grad: bfloat16 [262144, 128], P(('replica', 'mp')), may hold values from -6 to 6
Outputs:
- pooled: bfloat16 [262144, 128], P(('replica', 'mp'))
- new_table: float32 [65536, 128], P('mp')
- new_accum: float32 [65536, 128], P('mp')
The draws below stay inside these ranges and needn't reach their ends.
Inputs may be any that keep to these rules, and one draw needn't show every extreme that they name: `send_counts`: every device has one to 128 live slots for each owner; in every draw one owner has 128 live slots from every device.
All inputs are finite; a program needn't handle non-finite values.
Results may differ from the reference program's by a relative error of at most 0.0049.
Values may be sent and summed in bfloat16 or wider, within the bound.
A program may use at most 64 MiB of HBM per device.

```python
import math
import jax
import jax.numpy as jnp
import numpy as np
from jax import lax

EMBED = 128
ROWS_DEV = 2048
CAP = 128
BAG = 16
SENDERS = 1024
SAMPLES = 262144
ROWS = 65536
N_MP = 32


def draw_send_counts(key, part):
    key = jax.random.fold_in(key, 11)
    base_key, hot_key = jax.random.split(key)
    counts = jax.random.randint(base_key, (SENDERS, N_MP), 1, CAP + 1)
    hottest = jax.random.randint(hot_key, (), 0, N_MP)
    column = lax.broadcasted_iota(jnp.int32, (SENDERS, N_MP), 1)
    return jnp.where(column == hottest, CAP, counts).astype(jnp.int32)


def touch_ends(array, key, low, top_value):
    shape = array.shape
    place = [jax.random.randint(jax.random.fold_in(key, axis), (), 0, shape[axis]) for axis in range(len(shape))]
    array = array.at[tuple(place)].set(low)
    longest = shape.index(max(shape))
    place[longest] = (place[longest] + 1) % shape[longest]
    return array.at[tuple(place)].set(top_value)


def steps_of(key, shape, shards, smallest, largest):
    def one(axis_at, blocks):
        steps = jax.random.uniform(jax.random.fold_in(jax.random.fold_in(key, 6), axis_at), (blocks,), jnp.float32, smallest / len(shards), largest / len(shards))
        return jnp.repeat(jnp.exp(steps), shape[axis_at] // blocks).reshape((-1,) + (1,) * (len(shape) - axis_at - 1))

    gain = one(*shards[0])
    for cut in shards[1:]:
        gain = gain * one(*cut)
    return gain


def cumulative_ranks(amount, skew):
    portions = [(1 << 20) // math.isqrt(grade ** skew) + 1 for grade in range(1, amount + 1)]
    deviation = 1 + sum(portions) // (1 << 30)
    return np.cumsum(np.array([max(1, weight // deviation) for weight in portions]))


def ranked(stream_key, extent, number_of, lean):
    listing = cumulative_ranks(number_of, lean)
    pick = jax.random.randint(jax.random.fold_in(stream_key, 1), extent, 0, int(listing[number_of - 1]))
    standing = jnp.searchsorted(jnp.asarray(listing, jnp.int32), pick, side="right")
    return jax.random.permutation(jax.random.fold_in(stream_key, 2), number_of)[standing].astype(jnp.int32)


def bell_draw(key, shape, spread, most, pieces=(), held_as=jnp.bfloat16):
    result = jax.random.normal(key, shape, jnp.float32) * spread
    if len(pieces) > 0:
        result = steps_of(key, shape, pieces, -0.22, 0.18) * result
    return jnp.clip(result, min=-most, max=most).astype(held_as)


def setup_inputs(seed: int = 0) -> dict:
    keys = jax.random.split(jax.random.key(seed), 8)
    table = bell_draw(keys[0], (ROWS, EMBED), 0.5, 3.0, ((0, 32),), jnp.float32)
    accum = jnp.clip(jnp.exp(math.log(4.0) - 5.9914646 * jax.random.uniform(keys[1], (ROWS, EMBED), jnp.float32) ** steps_of(keys[1], (ROWS, EMBED), ((0, 32),), -0.2, 0.2)), 0.01, 4.0)
    request_ids = touch_ends(ranked(keys[2], (SENDERS, N_MP, CAP), ROWS_DEV, 2), jax.random.fold_in(keys[2], 3), 0, ROWS_DEV - 1).astype(jnp.int32)
    send_counts = draw_send_counts(jax.random.fold_in(keys[7], 71), 0)
    entry_slots = touch_ends(jax.random.randint(keys[4], (SAMPLES, BAG), 0, N_MP * CAP), jax.random.fold_in(keys[4], 1), 0, (N_MP * CAP) - 1).astype(jnp.int32)
    entry_weights = jnp.clip(jnp.exp(math.log(2.0) - 2.0794415 * jax.random.uniform(keys[5], (SAMPLES, BAG), jnp.float32) ** steps_of(keys[5], (SAMPLES, BAG), ((0, 1024),), -0.2, 0.2)), 0.25, 2.0).astype(jnp.bfloat16)
    pooled_grad = bell_draw(keys[6], (SAMPLES, EMBED), 1.0, 6.0, ((0, 1024),))
    return {"table": table, "accum": accum, "request_ids": request_ids, "send_counts": send_counts, "entry_slots": entry_slots, "entry_weights": entry_weights, "pooled_grad": pooled_grad}


def reference(table, accum, request_ids, send_counts, entry_slots, entry_weights, pooled_grad):
    senders = request_ids.shape[0]
    peers = request_ids.shape[1]
    capacity = request_ids.shape[2]
    bag_len = entry_slots.shape[1]
    per_dev = entry_slots.shape[0] // senders
    owner_base = (jnp.arange(peers, dtype=jnp.int32) * ROWS_DEV)[:, None]

    def one_device(carry, inputs):
        ids, counts, slots, weights, grads = inputs
        global_ids = (ids + owner_base).reshape(-1).astype(jnp.int32)
        rows = jnp.take(table, global_ids, axis=0).astype(jnp.bfloat16)
        live = (jnp.arange(capacity, dtype=jnp.int32)[None, :] < counts[:, None]).reshape(-1)
        scale = weights.astype(jnp.float32) * jnp.take(live, slots).astype(jnp.float32)
        picked = jnp.take(rows, slots, axis=0).astype(jnp.float32)
        pooled_dev = lax.optimization_barrier(jnp.sum(scale[:, :, None] * picked, axis=1)).astype(jnp.bfloat16)
        contrib = scale[:, :, None] * grads.astype(jnp.float32)[:, None, :]
        slot_grad = jax.ops.segment_sum(contrib.reshape(-1, EMBED), slots.reshape(-1), num_segments=peers * capacity)
        carry = carry.at[global_ids].add(slot_grad)
        return (carry, pooled_dev)
    inputs = (request_ids, send_counts, entry_slots.reshape(senders, per_dev, bag_len), entry_weights.reshape(senders, per_dev, bag_len), pooled_grad.reshape(senders, per_dev, EMBED))
    row_grad, pooled = lax.scan(one_device, jnp.zeros(table.shape, jnp.float32), inputs)
    new_accum = accum + row_grad * row_grad
    new_table = table - 0.5 * row_grad / jnp.sqrt(new_accum)
    return (pooled.reshape(senders * per_dev, EMBED), new_table, new_accum)
```

```python
import functools

import jax
import jax.numpy as jnp
from jax import lax
from jax.experimental import pallas as pl
from jax.experimental.pallas import tpu as pltpu
from jax.sharding import PartitionSpec as P

learn_rate = 0.5
FAR = 8
NEAR = 4
SIDE = 4
MESH = pl.DeviceIdType.MESH


def remote(src, dst, send_sem, recv_sem, r, z):
    return pltpu.make_async_remote_copy(
        src_ref=src, dst_ref=dst, send_sem=send_sem, recv_sem=recv_sem,
        device_id={"replica": r, "mp": z}, device_id_type=MESH,
    )


def place(index):
    return lax.rem(index, NEAR) * FAR + index // NEAR


class Seat:
    def __init__(self, n):
        self.n = n
        self.r, self.z = lax.axis_index("replica"), lax.axis_index("mp")
        self.x, self.y, self.c = self.r // (2 * SIDE), lax.rem(self.r // 2, SIDE), lax.rem(self.r, 2)
        self.a, self.b = self.z // NEAR, lax.rem(self.z, NEAR)
        self.twin = self.r + 1 - 2 * self.c

    def x_at(self, o):
        return lax.rem(self.x + o, SIDE)

    def y_at(self, o):
        return lax.rem(self.y + o, SIDE)

    def along_x(self, o):
        return (self.x_at(o) * SIDE + self.y) * 2 + self.c

    def along_y(self, o):
        return (self.x * SIDE + self.y_at(o)) * 2 + self.c

    def up(self, o):
        return lax.rem(self.z + o + self.n, self.n)

    def greet(self):
        barrier = pltpu.get_barrier_semaphore()

        def hello(r, z):
            pl.semaphore_signal(barrier, inc=1, device_id={"replica": r, "mp": z}, device_id_type=MESH)

        @pl.loop(1, SIDE)
        def _(o):
            hello(self.along_x(o), self.z)
            hello(self.along_y(o), self.z)

        @pl.loop(1, FAR)
        def _(o):
            hello(self.r, self.up(NEAR * o))

        hello(self.twin, self.z)
        for o in (-2, -1, 1, 2):
            hello(self.r, self.up(o))

        @pl.when(self.r != self.z)
        def _():
            hello(self.z, self.r)

        pl.semaphore_wait(barrier, 2 * (SIDE - 1) + FAR - 1 + 5 + jnp.where(self.r != self.z, 1, 0))

    def turn(self, src, dst, dst_local, sems):
        def away():
            return remote(src, dst, sems.at[0], sems.at[1], self.z, self.r)

        def here():
            return pltpu.make_async_copy(src, dst_local, sems.at[2])

        def start():
            @pl.when(self.r != self.z)
            def _():
                away().start()

            @pl.when(self.r == self.z)
            def _():
                here().start()

        def wait():
            @pl.when(self.r != self.z)
            def _():
                away().wait()

            @pl.when(self.r == self.z)
            def _():
                here().wait()

        return start, wait


def start_each(last, *copies):
    @pl.loop(1, last)
    def _(o):
        for copy in copies:
            copy(o).start()


def wait_each(last, *copies):
    @pl.loop(1, last)
    def _(o):
        for copy in copies:
            copy(o).wait()


def inward(n, piece_ref, ids_ref, grad_ref, table_out, ids_out, grad_out, ids_x, ids_y, grad_x, grad_y, grad_b,
           turn_sem, own_sem, far_send, far_recv, near_send, near_recv, id_send, id_recv, grad_send, grad_recv):
    seat = Seat(n)
    r, z, x, y, c = seat.r, seat.z, seat.x, seat.y, seat.c
    cut = grad_x.shape[3]
    low, high = pl.ds(0, cut), pl.ds(cut, cut)
    seat.greet()
    mine = table_out.at[place(z)]
    turn_start, turn_wait = seat.turn(piece_ref, table_out.at[place(r)], mine, turn_sem)
    turn_start()

    def ship(src, dst, k, to):
        return remote(src, dst, grad_send.at[k], grad_recv.at[k], to, z)

    def ship_ids(src, dst, k, to):
        return remote(src, dst, id_send.at[k], id_recv.at[k], to, z)

    def x_low(o):
        return ship(grad_ref.at[seat.x_at(o), :, :, low], grad_x.at[x], o, seat.along_x(o))

    def y_high(o):
        return ship(grad_ref.at[:, seat.y_at(o), :, high], grad_y.at[y], SIDE + o, seat.along_y(o))

    def y_low(o):
        return ship(grad_x.at[:, seat.y_at(o)], grad_b.at[y, :, :, low], 2 * SIDE + o, seat.along_y(o))

    def x_high(o):
        return ship(grad_y.at[:, seat.x_at(o)], grad_b.at[:, x, :, high], 3 * SIDE + o, seat.along_x(o))

    def x_ids(o):
        return ship_ids(ids_ref.at[seat.x_at(o)], ids_x.at[x], o, seat.along_x(o))

    def y_ids(o):
        return ship_ids(ids_x.at[:, seat.y_at(o)], ids_y.at[y], SIDE + o, seat.along_y(o))

    own = [pltpu.make_async_copy(src, dst, own_sem.at[k]) for k, (src, dst) in enumerate((
        (grad_ref.at[x, :, :, low], grad_x.at[x]),
        (grad_ref.at[:, y, :, high], grad_y.at[y]),
        (ids_ref.at[x], ids_x.at[x]),
        (grad_x.at[:, y], grad_b.at[y, :, :, low]),
        (grad_y.at[:, x], grad_b.at[:, x, :, high]),
        (ids_x.at[:, y], ids_y.at[y]),
        (grad_b.at[:, :, c], grad_out.at[c]),
        (ids_y.at[:, :, c], ids_out.at[c]),
    ))]
    start_each(SIDE, x_low, y_high, x_ids)
    for copy in own[:3]:
        copy.start()

    turn_wait()

    def far(o):
        return remote(mine, mine, far_send.at[o], far_recv.at[o], r, seat.up(NEAR * o))

    start_each(FAR, far)
    for copy in own[:3]:
        copy.wait()
    wait_each(SIDE, x_low, y_high, x_ids)
    start_each(SIDE, y_low, x_high, y_ids)
    for copy in own[3:6]:
        copy.start()
    wait_each(FAR, far)

    def near(k, first, count, o):
        block = table_out.at[pl.ds(seat.b * FAR + first, count)]
        return remote(block, block, near_send.at[k], near_recv.at[k], r, seat.up(o))

    half = FAR // 2
    nears = [near(0, 0, FAR, 1), near(1, 0, FAR, -1), near(2, 0, half, 2), near(3, half, half, -2)]
    for copy in nears:
        copy.start()
    for copy in own[3:6]:
        copy.wait()
    wait_each(SIDE, y_low, x_high, y_ids)
    twins = [ship(grad_b.at[:, :, 1 - c], grad_out.at[c], 0, seat.twin),
             ship_ids(ids_y.at[:, :, 1 - c], ids_out.at[c], 0, seat.twin)]
    for copy in twins + own[6:]:
        copy.start()
    for copy in twins + own[6:] + nears:
        copy.wait()


def outward(n, part_ref, rows_ref, rows_out, grad_out, rows_b, rows_y, rows_x, near_a, near_b, near_c, near_d,
            total, far_out, far_in, piece,
            turn_sem, own_sem, far_send, far_recv, near_send, near_recv, row_send, row_recv, fin_send, fin_recv):
    seat = Seat(n)
    r, z, x, y, c, b = seat.r, seat.z, seat.x, seat.y, seat.c, seat.b
    half = FAR // 2
    cut = rows_y.shape[3]
    low, high = pl.ds(0, cut), pl.ds(cut, cut)
    seat.greet()

    def near(k, first, count, o, dst):
        block = part_ref.at[lax.rem(b + o + NEAR, NEAR), pl.ds(first, count)]
        return remote(block, dst, near_send.at[k], near_recv.at[k], r, seat.up(o))

    nears = [near(0, 0, FAR, 1, near_a), near(1, 0, FAR, -1, near_b),
             near(2, 0, half, 2, near_c), near(3, half, half, -2, near_d)]
    for copy in nears:
        copy.start()

    def ship(src, dst, k, to):
        return remote(src, dst, row_send.at[k], row_recv.at[k], to, z)

    def y_low(o):
        return ship(rows_b.at[:, seat.y_at(o), :, low], rows_y.at[y], o, seat.along_y(o))

    def x_high(o):
        return ship(rows_b.at[:, :, seat.x_at(o), high], rows_x.at[x], SIDE + o, seat.along_x(o))

    def x_low(o):
        return ship(rows_y.at[:, :, seat.x_at(o)], rows_out.at[x, :, :, low], 2 * SIDE + o, seat.along_x(o))

    def y_high(o):
        return ship(rows_x.at[:, :, seat.y_at(o)], rows_out.at[:, y, :, high], 3 * SIDE + o, seat.along_y(o))

    own = [pltpu.make_async_copy(src, dst, own_sem.at[k]) for k, (src, dst) in enumerate((
        (rows_ref.at[c], rows_b.at[c]),
        (rows_b.at[:, y, :, low], rows_y.at[y]),
        (rows_b.at[:, :, x, high], rows_x.at[x]),
        (rows_y.at[:, :, x], rows_out.at[x, :, :, low]),
        (rows_x.at[:, :, y], rows_out.at[:, y, :, high]),
    ))]
    twin = ship(rows_ref.at[1 - c], rows_b.at[c], 0, seat.twin)
    twin.start()
    own[0].start()
    own[0].wait()
    twin.wait()
    start_each(SIDE, y_low, x_high)
    own[1].start()
    own[2].start()

    for copy in nears:
        copy.wait()
    for first, far_half in ((0, near_c), (half, near_d)):
        here = pl.ds(first, half)
        total[here] = (part_ref[b, here] + near_a[here]) + (near_b[here] + far_half[...])
    far_out[...] = total[...].astype(jnp.bfloat16)

    def far(o):
        return remote(far_out.at[lax.rem(seat.a + o, FAR)], far_in.at[o], far_send.at[o], far_recv.at[o],
                      r, seat.up(NEAR * o))

    start_each(FAR, far)
    own[1].wait()
    own[2].wait()
    wait_each(SIDE, y_low, x_high)
    start_each(SIDE, x_low, y_high)
    own[3].start()
    own[4].start()
    wait_each(FAR, far)
    far_sum = total[seat.a]
    for o in range(1, FAR):
        far_sum = far_sum + far_in[o].astype(jnp.float32)
    piece[...] = far_sum

    here = grad_out.at[x, y, c]
    afar = grad_out.at[z // (2 * SIDE), lax.rem(z // 2, SIDE), lax.rem(z, 2)]
    turn_start, turn_wait = seat.turn(piece, afar, here, turn_sem)
    turn_start()
    own[3].wait()
    own[4].wait()
    wait_each(SIDE, x_low, y_high)
    turn_wait()

    rows = piece.shape[0] // 2
    upper, lower = pl.ds(0, rows), pl.ds(rows, rows)

    def spread(ref, k, to):
        return remote(ref, ref, fin_send.at[k], fin_recv.at[k], to, z)

    def x_upper(o):
        return spread(grad_out.at[x, y, c, upper], o, seat.along_x(o))

    def y_lower(o):
        return spread(grad_out.at[x, y, c, lower], SIDE + o, seat.along_y(o))

    def y_upper(o):
        return spread(grad_out.at[:, y, c, upper], 2 * SIDE + o, seat.along_y(o))

    def x_lower(o):
        return spread(grad_out.at[x, :, c, lower], 3 * SIDE + o, seat.along_x(o))

    start_each(SIDE, x_upper, y_lower)
    wait_each(SIDE, x_upper, y_lower)
    start_each(SIDE, y_upper, x_lower)
    wait_each(SIDE, y_upper, x_lower)
    last = spread(grad_out.at[:, :, c], 0, seat.twin)
    last.start()
    last.wait()


SUB = 64


def incidence(capacity, counts_ref, slots_ref, weights_ref, cot_ref, inc_ref, grad_ref, hot):
    block, samples = inc_ref.shape
    bag = slots_ref.shape[0]
    step = pl.program_id(0)

    @pl.when(step == 0)
    def _():
        column = lax.broadcasted_iota(jnp.int32, (capacity, samples), 0)
        for entry in range(bag):
            low = lax.rem(slots_ref[entry:entry + 1, :], capacity)
            hot[entry] = jnp.where(column == low, 1.0, 0.0)

    @pl.loop(0, block // capacity)
    def _(part):
        owner = step * (block // capacity) + part
        weights = jnp.where(slots_ref[...] // capacity == owner, weights_ref[...].astype(jnp.float32), 0.0)
        for first in range(0, capacity, SUB):
            total = hot[0, first:first + SUB] * weights[0:1, :]
            for entry in range(1, bag):
                total += hot[entry, first:first + SUB] * weights[entry:entry + 1, :]
            slot = first + lax.broadcasted_iota(jnp.int32, (SUB, samples), 0)
            total = jnp.where(slot < counts_ref[owner], total, 0.0)
            here = pl.ds(pl.multiple_of(part * capacity + first, SUB), SUB)
            inc_ref[here, :] = total.astype(jnp.bfloat16)

    grad_ref[...] = jnp.dot(inc_ref[...], cot_ref[...], preferred_element_type=jnp.float32).astype(jnp.bfloat16)


def lookup_and_sum(ids_ref, grad_ref, table_ref, rows_ref, part_ref, pick, spread):
    group, _, capacity = ids_ref.shape
    half, width = table_ref.shape[0], table_ref.shape[1] // 2
    bf16 = jnp.bfloat16
    one, zero = jnp.ones((capacity, 128), bf16), jnp.zeros((capacity, 128), bf16)
    lane = lax.broadcasted_iota(jnp.int32, (capacity, 128), 1).astype(jnp.float32).astype(bf16)
    row = lax.broadcasted_iota(jnp.int32, (128, capacity), 0).astype(jnp.float32).astype(bf16)
    tops, doubled = [], []

    def split(ids):
        low = jnp.bitwise_and(ids, 127).astype(jnp.float32).astype(bf16)
        mid = jnp.bitwise_and(lax.shift_right_logical(ids, 7), half // 128 - 1).astype(jnp.float32).astype(bf16)
        return low, mid, ids >= half

    unit = 2 * half // (NEAR * FAR)

    for q in range(group):
        spot = ids_ref[q]
        spot = (lax.rem(spot // unit, NEAR) * FAR + spot // (unit * NEAR)) * unit + lax.rem(spot, unit)
        ids = jnp.broadcast_to(spot, (capacity, capacity))
        column = ids.astype(jnp.float32).T.astype(jnp.int32)
        here = slice(q * capacity, (q + 1) * capacity)
        low, mid, top = split(column)
        hot = jnp.where(lane == low, one, zero)
        for tile in range(half // 128):
            pick[here, tile * 128:(tile + 1) * 128] = jnp.where(mid == jnp.full_like(mid, tile), hot, zero)
        tops.append(top)
        cot = grad_ref[q].astype(jnp.float32)
        doubled.append(jnp.concatenate(
            [jnp.where(top, 0.0, cot).astype(bf16), jnp.where(top, cot, 0.0).astype(bf16)], axis=1))
        low, mid, _ = split(ids)
        hot = jnp.where(row == low, one, zero)
        for tile in range(half // 128):
            spread[tile * 128:(tile + 1) * 128, here] = jnp.where(mid == jnp.full_like(mid, tile), hot, zero)

    looked = jnp.dot(pick[...], table_ref[...], preferred_element_type=jnp.float32)
    for q in range(group):
        here = slice(q * capacity, (q + 1) * capacity)
        rows_ref[q] = jnp.where(tops[q], looked[here, width:], looked[here, :width]).astype(bf16)
    summed = jnp.dot(spread[...], jnp.concatenate(doubled, axis=0), preferred_element_type=jnp.float32)

    @pl.when(pl.program_id(0) == 0)
    def _():
        part_ref[0] = summed[:, :width]
        part_ref[1] = summed[:, width:]

    @pl.when(pl.program_id(0) > 0)
    def _():
        part_ref[0] += summed[:, :width]
        part_ref[1] += summed[:, width:]


def per_device(n, table, accum, request_ids, send_counts, entry_slots, entry_weights, pooled_grad):
    r = lax.axis_index("replica")
    rows, width = table.shape
    _, peers, capacity = request_ids.shape
    slots = peers * capacity
    samples, bag = entry_slots.shape
    unit = rows // n
    bf16, f32 = jnp.bfloat16, jnp.float32
    anywhere = pl.BlockSpec(memory_space=pl.ANY)
    vmem = pl.BlockSpec(memory_space=pltpu.VMEM)
    dma = pltpu.SemaphoreType.DMA
    by_owner = (SIDE, SIDE, 2)
    by_core = (2, SIDE, SIDE)
    by_y = (SIDE, SIDE, 2)

    block = 512
    inc, slot_grad = pl.pallas_call(
        functools.partial(incidence, capacity),
        grid=(slots // block,),
        in_specs=[
            pl.BlockSpec(memory_space=pltpu.SMEM),
            pl.BlockSpec((bag, samples), lambda i: (0, 0)),
            pl.BlockSpec((bag, samples), lambda i: (0, 0)),
            pl.BlockSpec((samples, width), lambda i: (0, 0)),
        ],
        out_specs=[pl.BlockSpec((block, samples), lambda i: (i, 0)), pl.BlockSpec((block, width), lambda i: (i, 0))],
        out_shape=[jax.ShapeDtypeStruct((slots, samples), bf16), jax.ShapeDtypeStruct((slots, width), bf16)],
        scratch_shapes=[pltpu.VMEM((bag, capacity, samples), f32)],
        name="incidence",
    )(send_counts.reshape(peers), entry_slots.T, entry_weights.T, pooled_grad)

    piece = lax.dynamic_slice(table, (r * unit, 0), (unit, width)).astype(bf16)
    whole, ids, grads = pl.pallas_call(
        functools.partial(inward, n),
        in_specs=[vmem, vmem, anywhere],
        out_specs=[vmem, vmem, anywhere],
        out_shape=[
            jax.ShapeDtypeStruct((n, unit, width), bf16),
            jax.ShapeDtypeStruct(by_core + (1, capacity), jnp.int32),
            jax.ShapeDtypeStruct(by_core + (capacity, width), bf16),
        ],
        scratch_shapes=[
            pltpu.VMEM(by_owner + (1, capacity), jnp.int32),
            pltpu.VMEM(by_y + (1, capacity), jnp.int32),
            pltpu.VMEM(by_owner + (capacity // 2, width), bf16),
            pltpu.VMEM(by_y + (capacity // 2, width), bf16),
            pltpu.VMEM(by_y + (capacity, width), bf16),
            dma((3,)), dma((8,)), dma((FAR,)), dma((FAR,)), dma((4,)), dma((4,)),
            dma((2 * SIDE,)), dma((2 * SIDE,)), dma((4 * SIDE,)), dma((4 * SIDE,)),
        ],
        compiler_params=pltpu.CompilerParams(collective_id=0, has_side_effects=True, vmem_limit_bytes=16 << 20),
        name="inward",
    )(piece, request_ids.reshape(by_owner + (1, capacity)), slot_grad.reshape(by_owner + (capacity, width)))

    group = 4
    halves = whole.reshape(2, rows // 2, width)
    looked, part = pl.pallas_call(
        lookup_and_sum,
        grid=(peers // group,),
        in_specs=[
            pl.BlockSpec((group, 1, capacity), lambda i: (i, 0, 0)),
            pl.BlockSpec((group, capacity, width), lambda i: (i, 0, 0)),
            pl.BlockSpec((rows // 2, 2 * width), lambda i: (0, 0)),
        ],
        out_specs=[
            pl.BlockSpec((group, capacity, width), lambda i: (i, 0, 0)),
            pl.BlockSpec((2, rows // 2, width), lambda i: (0, 0, 0)),
        ],
        out_shape=[
            jax.ShapeDtypeStruct((peers, capacity, width), bf16),
            jax.ShapeDtypeStruct((2, rows // 2, width), f32),
        ],
        scratch_shapes=[
            pltpu.VMEM((group * capacity, rows // 2), bf16),
            pltpu.VMEM((rows // 2, group * capacity), bf16),
        ],
        compiler_params=pltpu.CompilerParams(vmem_limit_bytes=32 << 20),
        name="lookup_and_sum",
    )(ids.reshape(peers, 1, capacity), grads.reshape(peers, capacity, width),
      jnp.concatenate([halves[0], halves[1]], axis=1))

    arrived, grad = pl.pallas_call(
        functools.partial(outward, n),
        in_specs=[vmem, anywhere],
        out_specs=[anywhere, vmem],
        out_shape=[
            jax.ShapeDtypeStruct(by_owner + (capacity, width), bf16),
            jax.ShapeDtypeStruct(by_owner + (unit, width), f32),
        ],
        scratch_shapes=[
            pltpu.VMEM(by_core + (capacity, width), bf16),
            pltpu.VMEM((SIDE, 2, SIDE, capacity // 2, width), bf16),
            pltpu.VMEM((SIDE, 2, SIDE, capacity // 2, width), bf16),
            pltpu.VMEM((FAR, unit, width), f32),
            pltpu.VMEM((FAR, unit, width), f32),
            pltpu.VMEM((FAR // 2, unit, width), f32),
            pltpu.VMEM((FAR // 2, unit, width), f32),
            pltpu.VMEM((FAR, unit, width), f32),
            pltpu.VMEM((FAR, unit, width), bf16),
            pltpu.VMEM((FAR, unit, width), bf16),
            pltpu.VMEM((unit, width), f32),
            dma((3,)), dma((5,)), dma((FAR,)), dma((FAR,)), dma((4,)), dma((4,)),
            dma((4 * SIDE,)), dma((4 * SIDE,)), dma((4 * SIDE,)), dma((4 * SIDE,)),
        ],
        compiler_params=pltpu.CompilerParams(collective_id=1, has_side_effects=True, vmem_limit_bytes=16 << 20),
        name="outward",
    )(part.reshape(NEAR, FAR, unit, width), looked.reshape(by_core + (capacity, width)))

    pooled = lax.dot_general(
        inc, arrived.reshape(slots, width), (((0,), (0,)), ((), ())), preferred_element_type=f32
    ).astype(bf16)
    grad = grad.reshape(rows, width)
    fresh = accum + grad * grad
    return pooled, table - learn_rate * grad / jnp.sqrt(fresh), fresh


def solution(mesh):
    n = mesh.shape["mp"]
    both = ("replica", "mp")
    return jax.shard_map(
        functools.partial(per_device, n),
        mesh=mesh,
        in_specs=(
            P("mp", None),
            P("mp", None),
            P(both, None, None),
            P(both, None),
            P(both, None),
            P(both, None),
            P(both, None),
        ),
        out_specs=(P(both, None), P("mp", None), P("mp", None)),
        check_vma=False,
    )
```

```python
import functools

import jax
import jax.numpy as jnp
from jax import lax
from jax.experimental import pallas as pl
from jax.experimental.pallas import tpu as pltpu
from jax.sharding import PartitionSpec as P

learn_rate = 0.5
FAR = 8
NEAR = 4
SIDE = 4
MESH = pl.DeviceIdType.MESH


def remote(src, dst, send_sem, recv_sem, r, z):
    return pltpu.make_async_remote_copy(
        src_ref=src, dst_ref=dst, send_sem=send_sem, recv_sem=recv_sem,
        device_id={"replica": r, "mp": z}, device_id_type=MESH,
    )


def place(index):
    return lax.rem(index, NEAR) * FAR + index // NEAR


class Seat:
    def __init__(self, n):
        self.n = n
        self.r, self.z = lax.axis_index("replica"), lax.axis_index("mp")
        self.x, self.y, self.c = self.r // (2 * SIDE), lax.rem(self.r // 2, SIDE), lax.rem(self.r, 2)
        self.a, self.b = self.z // NEAR, lax.rem(self.z, NEAR)
        self.twin = self.r + 1 - 2 * self.c

    def x_at(self, o):
        return lax.rem(self.x + o, SIDE)

    def y_at(self, o):
        return lax.rem(self.y + o, SIDE)

    def along_x(self, o):
        return (self.x_at(o) * SIDE + self.y) * 2 + self.c

    def along_y(self, o):
        return (self.x * SIDE + self.y_at(o)) * 2 + self.c

    def up(self, o):
        return lax.rem(self.z + o + self.n, self.n)

    def greet(self):
        barrier = pltpu.get_barrier_semaphore()

        def hello(r, z):
            pl.semaphore_signal(barrier, inc=1, device_id={"replica": r, "mp": z}, device_id_type=MESH)

        @pl.loop(1, SIDE)
        def _(o):
            hello(self.along_x(o), self.z)
            hello(self.along_y(o), self.z)

        @pl.loop(1, FAR)
        def _(o):
            hello(self.r, self.up(NEAR * o))

        hello(self.twin, self.z)
        for o in (-2, -1, 1, 2):
            hello(self.r, self.up(o))

        @pl.when(self.r != self.z)
        def _():
            hello(self.z, self.r)

        pl.semaphore_wait(barrier, 2 * (SIDE - 1) + FAR - 1 + 5 + jnp.where(self.r != self.z, 1, 0))

    def turn(self, src, dst, dst_local, sems):
        def away():
            return remote(src, dst, sems.at[0], sems.at[1], self.z, self.r)

        def here():
            return pltpu.make_async_copy(src, dst_local, sems.at[2])

        def start():
            @pl.when(self.r != self.z)
            def _():
                away().start()

            @pl.when(self.r == self.z)
            def _():
                here().start()

        def wait():
            @pl.when(self.r != self.z)
            def _():
                away().wait()

            @pl.when(self.r == self.z)
            def _():
                here().wait()

        return start, wait


def start_each(last, *copies):
    @pl.loop(1, last)
    def _(o):
        for copy in copies:
            copy(o).start()


def wait_each(last, *copies):
    @pl.loop(1, last)
    def _(o):
        for copy in copies:
            copy(o).wait()


SUB = 64
GROUP = 4


def step(n, counts_ref, piece_ref, ids_ref, slots_ref, weights_ref, cot_ref, inc_out, rows_out, grad_out,
         hot, inc, slot_grad, table, table_wide, ids_x, ids_y, ids_in, grad_x, grad_y, grad_b, grad_in,
         pick, spread, tops, doubled, part, looked, rows_b, rows_y, rows_x, near_a, near_b, near_c, near_d,
         total, far_out, far_in, piece,
         turn_sem, own_sem, far_sem, near_sem, id_sem, grad_sem, sum_sem, sum_far, row_sem, fin_sem):
    seat = Seat(n)
    r, z, x, y, c, b = seat.r, seat.z, seat.x, seat.y, seat.c, seat.b
    bf16, f32 = jnp.bfloat16, jnp.float32
    bag, capacity, samples = hot.shape
    width = cot_ref.shape[1]
    owners = inc.shape[0] // capacity
    middle, wide = FAR // 2, pick.shape[1]
    unit = piece.shape[0]
    low, high = pl.ds(0, capacity // 2), pl.ds(capacity // 2, capacity // 2)
    seat.greet()

    mine = table.at[place(z)]
    turn_start, turn_wait = seat.turn(piece_ref, table.at[place(r)], mine, turn_sem.at[0])
    turn_start()

    def far(o):
        return remote(mine, mine, far_sem.at[0, o], far_sem.at[1, o], r, seat.up(NEAR * o))

    def near(k, first, count, o):
        block = table.at[pl.ds(b * FAR + first, count)]
        return remote(block, block, near_sem.at[0, k], near_sem.at[1, k], r, seat.up(o))

    nears = [near(0, 0, FAR, 1), near(1, 0, FAR, -1), near(2, 0, middle, 2), near(3, middle, middle, -2)]

    def ship_ids(src, dst, k, to):
        return remote(src, dst, id_sem.at[0, k], id_sem.at[1, k], to, z)

    def x_ids(o):
        return ship_ids(ids_ref.at[seat.x_at(o)], ids_x.at[x], o, seat.along_x(o))

    def y_ids(o):
        return ship_ids(ids_x.at[:, seat.y_at(o)], ids_y.at[y], SIDE + o, seat.along_y(o))

    twin_ids = ship_ids(ids_y.at[:, :, 1 - c], ids_in.at[c], 0, seat.twin)

    def ship(src, dst, k, to):
        return remote(src, dst, grad_sem.at[0, k], grad_sem.at[1, k], to, z)

    def x_low(o):
        return ship(slot_grad.at[seat.x_at(o), :, :, low], grad_x.at[x], o, seat.along_x(o))

    def y_high(o):
        return ship(slot_grad.at[:, seat.y_at(o), :, high], grad_y.at[y], SIDE + o, seat.along_y(o))

    def y_low(o):
        return ship(grad_x.at[:, seat.y_at(o)], grad_b.at[y, :, :, low], 2 * SIDE + o, seat.along_y(o))

    def x_high(o):
        return ship(grad_y.at[:, seat.x_at(o)], grad_b.at[:, x, :, high], 3 * SIDE + o, seat.along_x(o))

    twin_grad = ship(grad_b.at[:, :, 1 - c], grad_in.at[c], 0, seat.twin)

    def ship_rows(src, dst, k, to):
        return remote(src, dst, row_sem.at[0, k], row_sem.at[1, k], to, z)

    def y_low_rows(o):
        return ship_rows(rows_b.at[:, seat.y_at(o), :, low], rows_y.at[y], o, seat.along_y(o))

    def x_high_rows(o):
        return ship_rows(rows_b.at[:, :, seat.x_at(o), high], rows_x.at[x], SIDE + o, seat.along_x(o))

    def x_low_rows(o):
        return ship_rows(rows_y.at[:, :, seat.x_at(o)], rows_out.at[x, :, :, low], 2 * SIDE + o, seat.along_x(o))

    def y_high_rows(o):
        return ship_rows(rows_x.at[:, :, seat.y_at(o)], rows_out.at[:, y, :, high], 3 * SIDE + o, seat.along_y(o))

    twin_rows = ship_rows(looked.at[1 - c], rows_b.at[c], 0, seat.twin)

    own = [pltpu.make_async_copy(src, dst, own_sem.at[k]) for k, (src, dst) in enumerate((
        (ids_ref.at[x], ids_x.at[x]),
        (ids_x.at[:, y], ids_y.at[y]),
        (ids_y.at[:, :, c], ids_in.at[c]),
        (slot_grad.at[x, :, :, low], grad_x.at[x]),
        (slot_grad.at[:, y, :, high], grad_y.at[y]),
        (grad_x.at[:, y], grad_b.at[y, :, :, low]),
        (grad_y.at[:, x], grad_b.at[:, x, :, high]),
        (grad_b.at[:, :, c], grad_in.at[c]),
        (looked.at[c], rows_b.at[c]),
        (rows_b.at[:, y, :, low], rows_y.at[y]),
        (rows_b.at[:, :, x, high], rows_x.at[x]),
        (rows_y.at[:, :, x], rows_out.at[x, :, :, low]),
        (rows_x.at[:, :, y], rows_out.at[:, y, :, high]),
        (inc, inc_out),
    ))]

    def start_own(*which):
        for k in which:
            own[k].start()

    def wait_own(*which):
        for k in which:
            own[k].wait()

    def incidence(first, last):
        @pl.loop(first, last)
        def _(owner):
            weights = jnp.where(slots_ref[...] // capacity == owner, weights_ref[...].astype(f32), 0.0)
            for at in range(0, capacity, SUB):
                acc = hot[0, at:at + SUB] * weights[0:1, :]
                for entry in range(1, bag):
                    acc += hot[entry, at:at + SUB] * weights[entry:entry + 1, :]
                slot = at + lax.broadcasted_iota(jnp.int32, (SUB, samples), 0)
                acc = jnp.where(slot < counts_ref[owner], acc, 0.0)
                inc[pl.ds(pl.multiple_of(owner * capacity + at, SUB), SUB), :] = acc.astype(bf16)

    def slot_sums(first, last):
        @pl.loop(first, last)
        def _(k):
            size = GROUP * capacity
            block = inc[pl.ds(pl.multiple_of(k * size, size), size), :]
            sums = jnp.dot(block, cot_ref[...], preferred_element_type=f32).astype(bf16)
            half_side = SIDE // 2
            slot_grad[k // half_side, pl.ds(lax.rem(k, half_side) * half_side, half_side)] = sums.reshape(
                half_side, 2, capacity, width)

    def masks(first, last):
        one, zero = jnp.ones((capacity, 128), bf16), jnp.zeros((capacity, 128), bf16)
        lane = lax.broadcasted_iota(jnp.int32, (capacity, 128), 1).astype(f32).astype(bf16)
        row = lax.broadcasted_iota(jnp.int32, (128, capacity), 0).astype(f32).astype(bf16)

        def split(ids):
            lows = jnp.bitwise_and(ids, 127).astype(f32).astype(bf16)
            mids = jnp.bitwise_and(lax.shift_right_logical(ids, 7), wide // 128 - 1).astype(f32).astype(bf16)
            return lows, mids

        @pl.loop(first, last)
        def _(q):
            spot = ids_in[q // (SIDE * SIDE), lax.rem(q // SIDE, SIDE), lax.rem(q, SIDE)]
            spot = (lax.rem(spot // unit, NEAR) * FAR + spot // (unit * NEAR)) * unit + lax.rem(spot, unit)
            ids = jnp.broadcast_to(spot, (capacity, capacity))
            column = ids.astype(f32).T.astype(jnp.int32)
            here = pl.ds(pl.multiple_of(q * capacity, capacity), capacity)
            lows, mids = split(column)
            lit = jnp.where(lane == lows, one, zero)
            for tile in range(wide // 128):
                pick[here, tile * 128:(tile + 1) * 128] = jnp.where(mids == jnp.full_like(mids, tile), lit, zero)
            tops[here, :] = jnp.where(column >= wide, 1.0, 0.0)
            lows, mids = split(ids)
            lit = jnp.where(row == lows, one, zero)
            for tile in range(wide // 128):
                spread[tile * 128:(tile + 1) * 128, here] = jnp.where(mids == jnp.full_like(mids, tile), lit, zero)

    def sum_rows():
        @pl.loop(0, owners)
        def _(q):
            here = pl.ds(pl.multiple_of(q * capacity, capacity), capacity)
            cot = grad_in[q // (SIDE * SIDE), lax.rem(q // SIDE, SIDE), lax.rem(q, SIDE)].astype(f32)
            top = tops[here, :] > 0.5
            doubled[here, 0:width] = jnp.where(top, 0.0, cot).astype(bf16)
            doubled[here, width:2 * width] = jnp.where(top, cot, 0.0).astype(bf16)

        for k in range(NEAR // 2):
            size = FAR * unit
            sums = jnp.dot(spread[k * size:(k + 1) * size, :], doubled[...], preferred_element_type=f32)
            part[k] = sums[:, :width].reshape(FAR, unit, width)
            part[k + NEAR // 2] = sums[:, width:].reshape(FAR, unit, width)

    def look_up():
        table_wide[:, 0:width] = table[0:owners // 2].reshape(wide, width)
        table_wide[:, width:2 * width] = table[owners // 2:owners].reshape(wide, width)

        @pl.loop(0, owners // GROUP)
        def _(k):
            size = GROUP * capacity
            here = pl.ds(pl.multiple_of(k * size, size), size)
            both = jnp.dot(pick[here, :], table_wide[...], preferred_element_type=f32)
            rows = jnp.where(tops[here, :] > 0.5, both[:, width:], both[:, :width]).astype(bf16)
            looked[k // SIDE, lax.rem(k, SIDE)] = rows.reshape(SIDE, capacity, width)

    start_each(SIDE, x_ids)
    start_own(0)
    low_slot = lax.broadcasted_iota(jnp.int32, (capacity, samples), 0)
    for entry in range(bag):
        hot[entry] = jnp.where(low_slot == lax.rem(slots_ref[entry:entry + 1, :], capacity), 1.0, 0.0)
    incidence(0, owners // 2)
    turn_wait()
    start_each(FAR, far)
    wait_own(0)
    wait_each(SIDE, x_ids)
    start_each(SIDE, y_ids)
    start_own(1)
    incidence(owners // 2, owners)
    slot_sums(0, owners // GROUP)
    start_each(SIDE, x_low, y_high)
    start_own(3, 4, 13)
    wait_own(1)
    wait_each(SIDE, y_ids)
    twin_ids.start()
    start_own(2)
    wait_own(2)
    twin_ids.wait()
    masks(0, owners // 2)
    wait_own(3, 4)
    wait_each(SIDE, x_low, y_high)
    start_each(SIDE, y_low, x_high)
    start_own(5, 6)
    wait_each(FAR, far)
    for copy in nears:
        copy.start()
    masks(owners // 2, owners)
    wait_own(5, 6)
    wait_each(SIDE, y_low, x_high)
    twin_grad.start()
    start_own(7)
    wait_own(7)
    twin_grad.wait()
    sum_rows()

    def sum_near(k, first, count, o, dst):
        block = part.at[lax.rem(b + o + NEAR, NEAR), pl.ds(first, count)]
        return remote(block, dst, sum_sem.at[0, k], sum_sem.at[1, k], r, seat.up(o))

    sum_nears = [sum_near(0, 0, FAR, 1, near_a), sum_near(1, 0, FAR, -1, near_b),
                 sum_near(2, 0, middle, 2, near_c), sum_near(3, middle, middle, -2, near_d)]

    def sum_far_copy(o):
        return remote(far_out.at[lax.rem(seat.a + o, FAR)], far_in.at[o], sum_far.at[0, o], sum_far.at[1, o],
                      r, seat.up(NEAR * o))

    for copy in sum_nears:
        copy.start()
    for copy in nears:
        copy.wait()
    look_up()
    twin_rows.start()
    start_own(8)
    wait_own(8)
    twin_rows.wait()
    start_each(SIDE, y_low_rows, x_high_rows)
    start_own(9, 10)
    for copy in sum_nears:
        copy.wait()
    for first, far_half in ((0, near_c), (middle, near_d)):
        here = pl.ds(first, middle)
        total[here] = (part[b, here] + near_a[here]) + (near_b[here] + far_half[...])
    far_out[...] = total[...].astype(bf16)
    start_each(FAR, sum_far_copy)
    wait_own(9, 10)
    wait_each(SIDE, y_low_rows, x_high_rows)
    start_each(SIDE, x_low_rows, y_high_rows)
    start_own(11, 12)
    wait_each(FAR, sum_far_copy)
    far_sum = total[seat.a]
    for o in range(1, FAR):
        far_sum = far_sum + far_in[o].astype(f32)
    piece[...] = far_sum

    afar = grad_out.at[z // (2 * SIDE), lax.rem(z // 2, SIDE), lax.rem(z, 2)]
    back_start, back_wait = seat.turn(piece, afar, grad_out.at[x, y, c], turn_sem.at[1])
    back_start()
    wait_own(11, 12, 13)
    wait_each(SIDE, x_low_rows, y_high_rows)
    back_wait()

    upper, lower = pl.ds(0, unit // 2), pl.ds(unit // 2, unit // 2)

    def share(ref, k, to):
        return remote(ref, ref, fin_sem.at[0, k], fin_sem.at[1, k], to, z)

    def x_upper(o):
        return share(grad_out.at[x, y, c, upper], o, seat.along_x(o))

    def y_lower(o):
        return share(grad_out.at[x, y, c, lower], SIDE + o, seat.along_y(o))

    def y_upper(o):
        return share(grad_out.at[:, y, c, upper], 2 * SIDE + o, seat.along_y(o))

    def x_lower(o):
        return share(grad_out.at[x, :, c, lower], 3 * SIDE + o, seat.along_x(o))

    start_each(SIDE, x_upper, y_lower)
    wait_each(SIDE, x_upper, y_lower)
    start_each(SIDE, y_upper, x_lower)
    wait_each(SIDE, y_upper, x_lower)
    last = share(grad_out.at[:, :, c], 0, seat.twin)
    last.start()
    last.wait()


def per_device(n, table, accum, request_ids, send_counts, entry_slots, entry_weights, pooled_grad):
    r = lax.axis_index("replica")
    rows, width = table.shape
    _, peers, capacity = request_ids.shape
    slots = peers * capacity
    samples, bag = entry_slots.shape
    unit = rows // n
    bf16, f32, i32 = jnp.bfloat16, jnp.float32, jnp.int32
    anywhere = pl.BlockSpec(memory_space=pl.ANY)
    vmem = pl.BlockSpec(memory_space=pltpu.VMEM)
    dma = pltpu.SemaphoreType.DMA
    by_owner = (SIDE, SIDE, 2)
    by_core = (2, SIDE, SIDE)
    by_line = (SIDE, 2, SIDE)
    cut = capacity // 2

    piece = lax.dynamic_slice(table, (r * unit, 0), (unit, width)).astype(bf16)
    inc, arrived, grad = pl.pallas_call(
        functools.partial(step, n),
        in_specs=[pl.BlockSpec(memory_space=pltpu.SMEM), vmem, vmem, vmem, vmem, vmem],
        out_specs=[anywhere, anywhere, vmem],
        out_shape=[
            jax.ShapeDtypeStruct((slots, samples), bf16),
            jax.ShapeDtypeStruct(by_owner + (capacity, width), bf16),
            jax.ShapeDtypeStruct(by_owner + (unit, width), f32),
        ],
        scratch_shapes=[
            pltpu.VMEM((bag, capacity, samples), f32),
            pltpu.VMEM((slots, samples), bf16),
            pltpu.VMEM(by_owner + (capacity, width), bf16),
            pltpu.VMEM((n, unit, width), bf16),
            pltpu.VMEM((rows // 2, 2 * width), bf16),
            pltpu.VMEM(by_owner + (1, capacity), i32),
            pltpu.VMEM(by_owner + (1, capacity), i32),
            pltpu.VMEM(by_core + (1, capacity), i32),
            pltpu.VMEM(by_owner + (cut, width), bf16),
            pltpu.VMEM(by_owner + (cut, width), bf16),
            pltpu.VMEM(by_owner + (capacity, width), bf16),
            pltpu.VMEM(by_core + (capacity, width), bf16),
            pltpu.VMEM((slots, rows // 2), bf16),
            pltpu.VMEM((rows // 2, slots), bf16),
            pltpu.VMEM((slots, width), f32),
            pltpu.VMEM((slots, 2 * width), bf16),
            pltpu.VMEM((NEAR, FAR, unit, width), f32),
            pltpu.VMEM(by_core + (capacity, width), bf16),
            pltpu.VMEM(by_core + (capacity, width), bf16),
            pltpu.VMEM(by_line + (cut, width), bf16),
            pltpu.VMEM(by_line + (cut, width), bf16),
            pltpu.VMEM((FAR, unit, width), f32),
            pltpu.VMEM((FAR, unit, width), f32),
            pltpu.VMEM((FAR // 2, unit, width), f32),
            pltpu.VMEM((FAR // 2, unit, width), f32),
            pltpu.VMEM((FAR, unit, width), f32),
            pltpu.VMEM((FAR, unit, width), bf16),
            pltpu.VMEM((FAR, unit, width), bf16),
            pltpu.VMEM((unit, width), f32),
            dma((2, 3)), dma((14,)), dma((2, FAR)), dma((2, 4)), dma((2, 2 * SIDE)), dma((2, 4 * SIDE)),
            dma((2, 4)), dma((2, FAR)), dma((2, 4 * SIDE)), dma((2, 4 * SIDE)),
        ],
        compiler_params=pltpu.CompilerParams(collective_id=0, has_side_effects=True, vmem_limit_bytes=48 << 20),
        name="step",
    )(send_counts.reshape(peers), piece, request_ids.reshape(by_owner + (1, capacity)),
      entry_slots.T, entry_weights.T, pooled_grad)

    pooled = lax.dot_general(
        inc, arrived.reshape(slots, width), (((0,), (0,)), ((), ())), preferred_element_type=f32
    ).astype(bf16)
    grad = grad.reshape(rows, width)
    fresh = accum + grad * grad
    return pooled, table - learn_rate * grad / jnp.sqrt(fresh), fresh


def solution(mesh):
    n = mesh.shape["mp"]
    both = ("replica", "mp")
    return jax.shard_map(
        functools.partial(per_device, n),
        mesh=mesh,
        in_specs=(
            P("mp", None),
            P("mp", None),
            P(both, None, None),
            P(both, None),
            P(both, None),
            P(both, None),
            P(both, None),
        ),
        out_specs=(P(both, None), P("mp", None), P("mp", None)),
        check_vma=False,
    )
```

```python
import functools

import jax
import jax.numpy as jnp
from jax import lax
from jax.experimental import pallas as pl
from jax.experimental.pallas import tpu as pltpu
from jax.sharding import PartitionSpec as P

learn_rate = 0.5
FAR = 8
NEAR = 4
SIDE = 4
MESH = pl.DeviceIdType.MESH


def remote(src, dst, send_sem, recv_sem, r, z):
    return pltpu.make_async_remote_copy(
        src_ref=src, dst_ref=dst, send_sem=send_sem, recv_sem=recv_sem,
        device_id={"replica": r, "mp": z}, device_id_type=MESH,
    )


def place(index):
    return lax.rem(index, NEAR) * FAR + index // NEAR


class Seat:
    def __init__(self, n):
        self.n = n
        self.r, self.z = lax.axis_index("replica"), lax.axis_index("mp")
        self.x, self.y, self.c = self.r // (2 * SIDE), lax.rem(self.r // 2, SIDE), lax.rem(self.r, 2)
        self.a, self.b = self.z // NEAR, lax.rem(self.z, NEAR)
        self.twin = self.r + 1 - 2 * self.c

    def x_at(self, o):
        return lax.rem(self.x + o, SIDE)

    def y_at(self, o):
        return lax.rem(self.y + o, SIDE)

    def along_x(self, o):
        return (self.x_at(o) * SIDE + self.y) * 2 + self.c

    def along_y(self, o):
        return (self.x * SIDE + self.y_at(o)) * 2 + self.c

    def up(self, o):
        return lax.rem(self.z + o + self.n, self.n)

    def greet(self):
        barrier = pltpu.get_barrier_semaphore()

        def hello(r, z):
            pl.semaphore_signal(barrier, inc=1, device_id={"replica": r, "mp": z}, device_id_type=MESH)

        @pl.loop(1, SIDE)
        def _(o):
            hello(self.along_x(o), self.z)
            hello(self.along_y(o), self.z)

        @pl.loop(1, FAR)
        def _(o):
            hello(self.r, self.up(NEAR * o))

        hello(self.twin, self.z)
        for o in (-2, -1, 1, 2):
            hello(self.r, self.up(o))

        @pl.when(self.r != self.z)
        def _():
            hello(self.z, self.r)

        pl.semaphore_wait(barrier, 2 * (SIDE - 1) + FAR - 1 + 5 + jnp.where(self.r != self.z, 1, 0))

    def turn(self, src, dst, dst_local, sems):
        def away():
            return remote(src, dst, sems.at[0], sems.at[1], self.z, self.r)

        def here():
            return pltpu.make_async_copy(src, dst_local, sems.at[2])

        def start():
            @pl.when(self.r != self.z)
            def _():
                away().start()

            @pl.when(self.r == self.z)
            def _():
                here().start()

        def wait():
            @pl.when(self.r != self.z)
            def _():
                away().wait()

            @pl.when(self.r == self.z)
            def _():
                here().wait()

        return start, wait


def start_each(last, *copies):
    @pl.loop(1, last)
    def _(o):
        for copy in copies:
            copy(o).start()


def wait_each(last, *copies):
    @pl.loop(1, last)
    def _(o):
        for copy in copies:
            copy(o).wait()


SUB = 64
PACK = 16
GROUP = 4


def step(n, counts_ref, table_ref, ids_ref, slots_hbm, weights_hbm, cot_hbm, pooled_out, grad_out,
         fetched, piece_ref, slots_ref, weights_ref, cot_ref, hot, inc, slot_grad, table, table_wide, ids_x, ids_y, ids_in, grad_x, grad_y, grad_b, grad_in,
         pick, spread, tops, doubled, part, looked, rows_out, rows_b, rows_y, rows_x, near_a, near_b, near_c, near_d,
         total, far_out, far_in, piece,
         turn_sem, own_sem, far_sem, near_sem, id_sem, grad_sem, sum_sem, sum_far, row_sem, fin_sem, fetch_sem):
    seat = Seat(n)
    r, z, x, y, c, b = seat.r, seat.z, seat.x, seat.y, seat.c, seat.b
    bf16, f32 = jnp.bfloat16, jnp.float32
    bag, samples = slots_ref.shape
    capacity = hot.shape[1] * PACK
    width = cot_ref.shape[1]
    owners = inc.shape[0] // capacity
    middle, wide = FAR // 2, pick.shape[1]
    unit = piece.shape[0]
    low, high = pl.ds(0, capacity // 2), pl.ds(capacity // 2, capacity // 2)
    fetches = [pltpu.make_async_copy(src, dst, fetch_sem.at[k]) for k, (src, dst) in enumerate((
        (table_ref.at[pl.ds(pl.multiple_of(r * unit, unit), unit)], fetched),
        (slots_hbm, slots_ref),
        (weights_hbm, weights_ref),
        (cot_hbm, cot_ref),
    ))]
    for fetch in fetches:
        fetch.start()
    seat.greet()
    for fetch in fetches:
        fetch.wait()
    piece_ref[...] = fetched[...].astype(bf16)

    mine = table.at[place(z)]
    turn_start, turn_wait = seat.turn(piece_ref, table.at[place(r)], mine, turn_sem.at[0])
    turn_start()

    def far(o):
        return remote(mine, mine, far_sem.at[0, o], far_sem.at[1, o], r, seat.up(NEAR * o))

    def near(k, first, count, o):
        block = table.at[pl.ds(b * FAR + first, count)]
        return remote(block, block, near_sem.at[0, k], near_sem.at[1, k], r, seat.up(o))

    nears = [near(0, 0, FAR, 1), near(1, 0, FAR, -1), near(2, 0, middle, 2), near(3, middle, middle, -2)]

    def ship_ids(src, dst, k, to):
        return remote(src, dst, id_sem.at[0, k], id_sem.at[1, k], to, z)

    def x_ids(o):
        return ship_ids(ids_ref.at[seat.x_at(o)], ids_x.at[x], o, seat.along_x(o))

    def y_ids(o):
        return ship_ids(ids_x.at[:, seat.y_at(o)], ids_y.at[y], SIDE + o, seat.along_y(o))

    twin_ids = ship_ids(ids_y.at[:, :, 1 - c], ids_in.at[c], 0, seat.twin)

    def ship(src, dst, k, to):
        return remote(src, dst, grad_sem.at[0, k], grad_sem.at[1, k], to, z)

    def x_low(o):
        return ship(slot_grad.at[seat.x_at(o), :, :, low], grad_x.at[x], o, seat.along_x(o))

    def y_high(o):
        return ship(slot_grad.at[:, seat.y_at(o), :, high], grad_y.at[y], SIDE + o, seat.along_y(o))

    def y_low(o):
        return ship(grad_x.at[:, seat.y_at(o)], grad_b.at[y, :, :, low], 2 * SIDE + o, seat.along_y(o))

    def x_high(o):
        return ship(grad_y.at[:, seat.x_at(o)], grad_b.at[:, x, :, high], 3 * SIDE + o, seat.along_x(o))

    twin_grad = ship(grad_b.at[:, :, 1 - c], grad_in.at[c], 0, seat.twin)

    def ship_rows(src, dst, k, to):
        return remote(src, dst, row_sem.at[0, k], row_sem.at[1, k], to, z)

    def y_low_rows(o):
        return ship_rows(rows_b.at[:, seat.y_at(o), :, low], rows_y.at[y], o, seat.along_y(o))

    def x_high_rows(o):
        return ship_rows(rows_b.at[:, :, seat.x_at(o), high], rows_x.at[x], SIDE + o, seat.along_x(o))

    def x_low_rows(o):
        return ship_rows(rows_y.at[:, :, seat.x_at(o)], rows_out.at[x, :, :, low], 2 * SIDE + o, seat.along_x(o))

    def y_high_rows(o):
        return ship_rows(rows_x.at[:, :, seat.y_at(o)], rows_out.at[:, y, :, high], 3 * SIDE + o, seat.along_y(o))

    twin_rows = ship_rows(looked.at[1 - c], rows_b.at[c], 0, seat.twin)

    own = [pltpu.make_async_copy(src, dst, own_sem.at[k]) for k, (src, dst) in enumerate((
        (ids_ref.at[x], ids_x.at[x]),
        (ids_x.at[:, y], ids_y.at[y]),
        (ids_y.at[:, :, c], ids_in.at[c]),
        (slot_grad.at[x, :, :, low], grad_x.at[x]),
        (slot_grad.at[:, y, :, high], grad_y.at[y]),
        (grad_x.at[:, y], grad_b.at[y, :, :, low]),
        (grad_y.at[:, x], grad_b.at[:, x, :, high]),
        (grad_b.at[:, :, c], grad_in.at[c]),
        (looked.at[c], rows_b.at[c]),
        (rows_b.at[:, y, :, low], rows_y.at[y]),
        (rows_b.at[:, :, x, high], rows_x.at[x]),
        (rows_y.at[:, :, x], rows_out.at[x, :, :, low]),
        (rows_x.at[:, :, y], rows_out.at[:, y, :, high]),
    ))]

    def start_own(*which):
        for k in which:
            own[k].start()

    def wait_own(*which):
        for k in which:
            own[k].wait()

    def incidence(first, last):
        tiles = SUB // PACK

        @pl.loop(first, last)
        def _(owner):
            weights = jnp.where(slots_ref[...] // capacity == owner, weights_ref[...].astype(f32), 0.0)
            scales = [jnp.broadcast_to(weights[entry:entry + 1, :], (PACK, samples)).astype(bf16)[None]
                      for entry in range(bag)]

            def entries(at, lower, upper):
                if upper - lower == 1:
                    return hot[lower, at:at + tiles] * scales[lower]
                middle_entry = (lower + upper) // 2
                return entries(at, lower, middle_entry) + entries(at, middle_entry, upper)

            for at in range(0, capacity // PACK, tiles):
                slot = at * PACK + lax.broadcasted_iota(jnp.int32, (SUB, samples), 0)
                acc = entries(at, 0, bag).reshape(SUB, samples).astype(f32)
                acc = jnp.where(slot < counts_ref[owner], acc, 0.0)
                inc[pl.ds(pl.multiple_of(owner * capacity + at * PACK, SUB), SUB), :] = acc.astype(bf16)

    def slot_sums(first, last):
        @pl.loop(first, last)
        def _(k):
            size = GROUP * capacity
            block = inc[pl.ds(pl.multiple_of(k * size, size), size), :]
            sums = jnp.dot(block, cot_ref[...], preferred_element_type=f32).astype(bf16)
            half_side = SIDE // 2
            slot_grad[k // half_side, pl.ds(lax.rem(k, half_side) * half_side, half_side)] = sums.reshape(
                half_side, 2, capacity, width)

    def masks(first, last):
        one, zero = jnp.ones((capacity, 128), bf16), jnp.zeros((capacity, 128), bf16)
        lane = lax.broadcasted_iota(jnp.int32, (capacity, 128), 1).astype(f32).astype(bf16)
        row = lax.broadcasted_iota(jnp.int32, (128, capacity), 0).astype(f32).astype(bf16)

        def split(ids):
            lows = jnp.bitwise_and(ids, 127).astype(f32).astype(bf16)
            mids = jnp.bitwise_and(lax.shift_right_logical(ids, 7), wide // 128 - 1).astype(f32).astype(bf16)
            return lows, mids

        @pl.loop(first, last)
        def _(q):
            spot = ids_in[q // (SIDE * SIDE), lax.rem(q // SIDE, SIDE), lax.rem(q, SIDE)]
            spot = (lax.rem(spot // unit, NEAR) * FAR + spot // (unit * NEAR)) * unit + lax.rem(spot, unit)
            ids = jnp.broadcast_to(spot, (capacity, capacity))
            column = ids.astype(f32).T.astype(jnp.int32)
            here = pl.ds(pl.multiple_of(q * capacity, capacity), capacity)
            lows, mids = split(column)
            lit = jnp.where(lane == lows, one, zero)
            for tile in range(wide // 128):
                pick[here, tile * 128:(tile + 1) * 128] = jnp.where(mids == jnp.full_like(mids, tile), lit, zero)
            tops[here, :] = jnp.where(column >= wide, 1.0, 0.0)
            lows, mids = split(ids)
            lit = jnp.where(row == lows, one, zero)
            for tile in range(wide // 128):
                spread[tile * 128:(tile + 1) * 128, here] = jnp.where(mids == jnp.full_like(mids, tile), lit, zero)

    def sum_rows():
        @pl.loop(0, owners)
        def _(q):
            here = pl.ds(pl.multiple_of(q * capacity, capacity), capacity)
            cot = grad_in[q // (SIDE * SIDE), lax.rem(q // SIDE, SIDE), lax.rem(q, SIDE)].astype(f32)
            top = tops[here, :] > 0.5
            doubled[here, 0:width] = jnp.where(top, 0.0, cot).astype(bf16)
            doubled[here, width:2 * width] = jnp.where(top, cot, 0.0).astype(bf16)

        for k in range(NEAR // 2):
            size = FAR * unit
            sums = jnp.dot(spread[k * size:(k + 1) * size, :], doubled[...], preferred_element_type=f32)
            part[k] = sums[:, :width].reshape(FAR, unit, width)
            part[k + NEAR // 2] = sums[:, width:].reshape(FAR, unit, width)

    def look_up():
        table_wide[:, 0:width] = table[0:owners // 2].reshape(wide, width)
        table_wide[:, width:2 * width] = table[owners // 2:owners].reshape(wide, width)

        @pl.loop(0, owners // GROUP)
        def _(k):
            size = GROUP * capacity
            here = pl.ds(pl.multiple_of(k * size, size), size)
            both = jnp.dot(pick[here, :], table_wide[...], preferred_element_type=f32)
            rows = jnp.where(tops[here, :] > 0.5, both[:, width:], both[:, :width]).astype(bf16)
            looked[k // SIDE, lax.rem(k, SIDE)] = rows.reshape(SIDE, capacity, width)

    def pool():
        def add(k, acc):
            size = 2 * GROUP * capacity
            block = inc[pl.ds(pl.multiple_of(k * size, size), size), :]
            rows = rows_out[k].reshape(size, width)
            return acc + lax.dot_general(block, rows, (((0,), (0,)), ((), ())), preferred_element_type=f32)

        pooled = lax.fori_loop(0, SIDE, add, jnp.zeros((samples, width), f32))
        pooled_out[...] = pooled.astype(bf16)

    start_each(SIDE, x_ids)
    start_own(0)
    low_slot = lax.broadcasted_iota(jnp.int32, (capacity, samples), 0)
    for entry in range(bag):
        lit = jnp.where(low_slot == lax.rem(slots_ref[entry:entry + 1, :], capacity), 1.0, 0.0)
        hot[entry] = lit.astype(bf16).reshape(capacity // PACK, PACK, samples)
    incidence(0, owners // 2)
    turn_wait()
    start_each(FAR, far)
    wait_own(0)
    wait_each(SIDE, x_ids)
    start_each(SIDE, y_ids)
    start_own(1)
    incidence(owners // 2, owners)
    slot_sums(0, owners // GROUP)
    start_each(SIDE, x_low, y_high)
    start_own(3, 4)
    wait_own(1)
    wait_each(SIDE, y_ids)
    twin_ids.start()
    start_own(2)
    wait_own(2)
    twin_ids.wait()
    masks(0, owners // 2)
    wait_own(3, 4)
    wait_each(SIDE, x_low, y_high)
    start_each(SIDE, y_low, x_high)
    start_own(5, 6)
    wait_each(FAR, far)
    for copy in nears:
        copy.start()
    masks(owners // 2, owners)
    wait_own(5, 6)
    wait_each(SIDE, y_low, x_high)
    twin_grad.start()
    start_own(7)
    wait_own(7)
    twin_grad.wait()
    sum_rows()

    def sum_near(k, first, count, o, dst):
        block = part.at[lax.rem(b + o + NEAR, NEAR), pl.ds(first, count)]
        return remote(block, dst, sum_sem.at[0, k], sum_sem.at[1, k], r, seat.up(o))

    sum_nears = [sum_near(0, 0, FAR, 1, near_a), sum_near(1, 0, FAR, -1, near_b),
                 sum_near(2, 0, middle, 2, near_c), sum_near(3, middle, middle, -2, near_d)]

    def sum_far_copy(o):
        return remote(far_out.at[lax.rem(seat.a + o, FAR)], far_in.at[o], sum_far.at[0, o], sum_far.at[1, o],
                      r, seat.up(NEAR * o))

    for copy in sum_nears:
        copy.start()
    for copy in nears:
        copy.wait()
    look_up()
    twin_rows.start()
    start_own(8)
    wait_own(8)
    twin_rows.wait()
    start_each(SIDE, y_low_rows, x_high_rows)
    start_own(9, 10)
    for copy in sum_nears:
        copy.wait()
    for first, far_half in ((0, near_c), (middle, near_d)):
        here = pl.ds(first, middle)
        total[here] = (part[b, here] + near_a[here]) + (near_b[here] + far_half[...])
    far_out[...] = total[...].astype(bf16)
    start_each(FAR, sum_far_copy)
    wait_own(9, 10)
    wait_each(SIDE, y_low_rows, x_high_rows)
    start_each(SIDE, x_low_rows, y_high_rows)
    start_own(11, 12)
    wait_each(FAR, sum_far_copy)
    far_sum = total[seat.a]
    for o in range(1, FAR):
        far_sum = far_sum + far_in[o].astype(f32)
    piece[...] = far_sum

    afar = grad_out.at[z // (2 * SIDE), lax.rem(z // 2, SIDE), lax.rem(z, 2)]
    back_start, back_wait = seat.turn(piece, afar, grad_out.at[x, y, c], turn_sem.at[1])
    back_start()
    wait_own(11, 12)
    wait_each(SIDE, x_low_rows, y_high_rows)
    pool()
    back_wait()

    upper, lower = pl.ds(0, unit // 2), pl.ds(unit // 2, unit // 2)

    def share(ref, k, to):
        return remote(ref, ref, fin_sem.at[0, k], fin_sem.at[1, k], to, z)

    def x_upper(o):
        return share(grad_out.at[x, y, c, upper], o, seat.along_x(o))

    def y_lower(o):
        return share(grad_out.at[x, y, c, lower], SIDE + o, seat.along_y(o))

    def y_upper(o):
        return share(grad_out.at[:, y, c, upper], 2 * SIDE + o, seat.along_y(o))

    def x_lower(o):
        return share(grad_out.at[x, :, c, lower], 3 * SIDE + o, seat.along_x(o))

    start_each(SIDE, x_upper, y_lower)
    wait_each(SIDE, x_upper, y_lower)
    start_each(SIDE, y_upper, x_lower)
    wait_each(SIDE, y_upper, x_lower)
    last = share(grad_out.at[:, :, c], 0, seat.twin)
    last.start()
    last.wait()


def per_device(n, table, accum, request_ids, send_counts, entry_slots, entry_weights, pooled_grad):
    rows, width = table.shape
    _, peers, capacity = request_ids.shape
    slots = peers * capacity
    samples, bag = entry_slots.shape
    unit = rows // n
    bf16, f32, i32 = jnp.bfloat16, jnp.float32, jnp.int32
    vmem = pl.BlockSpec(memory_space=pltpu.VMEM)
    hbm = pl.BlockSpec(memory_space=pltpu.HBM)
    dma = pltpu.SemaphoreType.DMA
    by_owner = (SIDE, SIDE, 2)
    by_core = (2, SIDE, SIDE)
    by_line = (SIDE, 2, SIDE)
    cut = capacity // 2

    pooled, grad = pl.pallas_call(
        functools.partial(step, n),
        in_specs=[pl.BlockSpec(memory_space=pltpu.SMEM), hbm, hbm, hbm, hbm, hbm],
        out_specs=[vmem, vmem],
        out_shape=[
            jax.ShapeDtypeStruct((samples, width), bf16),
            jax.ShapeDtypeStruct(by_owner + (unit, width), f32),
        ],
        scratch_shapes=[
            pltpu.VMEM((unit, width), f32),
            pltpu.VMEM((unit, width), bf16),
            pltpu.VMEM((bag, samples), i32),
            pltpu.VMEM((bag, samples), bf16),
            pltpu.VMEM((samples, width), bf16),
            pltpu.VMEM((bag, capacity // PACK, PACK, samples), bf16),
            pltpu.VMEM((slots, samples), bf16),
            pltpu.VMEM(by_owner + (capacity, width), bf16),
            pltpu.VMEM((n, unit, width), bf16),
            pltpu.VMEM((rows // 2, 2 * width), bf16),
            pltpu.VMEM(by_owner + (1, capacity), i32),
            pltpu.VMEM(by_owner + (1, capacity), i32),
            pltpu.VMEM(by_core + (1, capacity), i32),
            pltpu.VMEM(by_owner + (cut, width), bf16),
            pltpu.VMEM(by_owner + (cut, width), bf16),
            pltpu.VMEM(by_owner + (capacity, width), bf16),
            pltpu.VMEM(by_core + (capacity, width), bf16),
            pltpu.VMEM((slots, rows // 2), bf16),
            pltpu.VMEM((rows // 2, slots), bf16),
            pltpu.VMEM((slots, width), f32),
            pltpu.VMEM((slots, 2 * width), bf16),
            pltpu.VMEM((NEAR, FAR, unit, width), f32),
            pltpu.VMEM(by_core + (capacity, width), bf16),
            pltpu.VMEM(by_owner + (capacity, width), bf16),
            pltpu.VMEM(by_core + (capacity, width), bf16),
            pltpu.VMEM(by_line + (cut, width), bf16),
            pltpu.VMEM(by_line + (cut, width), bf16),
            pltpu.VMEM((FAR, unit, width), f32),
            pltpu.VMEM((FAR, unit, width), f32),
            pltpu.VMEM((FAR // 2, unit, width), f32),
            pltpu.VMEM((FAR // 2, unit, width), f32),
            pltpu.VMEM((FAR, unit, width), f32),
            pltpu.VMEM((FAR, unit, width), bf16),
            pltpu.VMEM((FAR, unit, width), bf16),
            pltpu.VMEM((unit, width), f32),
            dma((2, 3)), dma((13,)), dma((2, FAR)), dma((2, 4)), dma((2, 2 * SIDE)), dma((2, 4 * SIDE)),
            dma((2, 4)), dma((2, FAR)), dma((2, 4 * SIDE)), dma((2, 4 * SIDE)), dma((4,)),
        ],
        compiler_params=pltpu.CompilerParams(collective_id=0, has_side_effects=True, vmem_limit_bytes=63400000),
        name="step",
    )(send_counts.reshape(peers), table, request_ids.reshape(by_owner + (1, capacity)),
      entry_slots.T, entry_weights.T, pooled_grad)

    grad = grad.reshape(rows, width)
    fresh = accum + grad * grad
    return pooled, table - learn_rate * grad / jnp.sqrt(fresh), fresh


def solution(mesh):
    n = mesh.shape["mp"]
    both = ("replica", "mp")
    return jax.shard_map(
        functools.partial(per_device, n),
        mesh=mesh,
        in_specs=(
            P("mp", None),
            P("mp", None),
            P(both, None, None),
            P(both, None),
            P(both, None),
            P(both, None),
            P(both, None),
        ),
        out_specs=(P(both, None), P("mp", None), P("mp", None)),
        check_vma=False,
    )
```

```python
import functools

import jax
import jax.numpy as jnp
from jax import lax
from jax.experimental import pallas as pl
from jax.experimental.pallas import tpu as pltpu
from jax.sharding import PartitionSpec as P

learn_rate = 0.5
FAR = 8
NEAR = 4
SIDE = 4
MESH = pl.DeviceIdType.MESH


def remote(src, dst, send_sem, recv_sem, r, z):
    return pltpu.make_async_remote_copy(
        src_ref=src, dst_ref=dst, send_sem=send_sem, recv_sem=recv_sem,
        device_id={"replica": r, "mp": z}, device_id_type=MESH,
    )


def place(index):
    return lax.rem(index, NEAR) * FAR + index // NEAR


class Seat:
    def __init__(self, n):
        self.n = n
        self.r, self.z = lax.axis_index("replica"), lax.axis_index("mp")
        self.x, self.y, self.c = self.r // (2 * SIDE), lax.rem(self.r // 2, SIDE), lax.rem(self.r, 2)
        self.a, self.b = self.z // NEAR, lax.rem(self.z, NEAR)
        self.twin = self.r + 1 - 2 * self.c

    def x_at(self, o):
        return lax.rem(self.x + o, SIDE)

    def y_at(self, o):
        return lax.rem(self.y + o, SIDE)

    def along_x(self, o):
        return (self.x_at(o) * SIDE + self.y) * 2 + self.c

    def along_y(self, o):
        return (self.x * SIDE + self.y_at(o)) * 2 + self.c

    def up(self, o):
        return lax.rem(self.z + o + self.n, self.n)

    def greet(self):
        barrier = pltpu.get_barrier_semaphore()

        def hello(r, z):
            pl.semaphore_signal(barrier, inc=1, device_id={"replica": r, "mp": z}, device_id_type=MESH)

        @pl.loop(1, SIDE)
        def _(o):
            hello(self.along_x(o), self.z)
            hello(self.along_y(o), self.z)

        @pl.loop(1, FAR)
        def _(o):
            hello(self.r, self.up(NEAR * o))

        hello(self.twin, self.z)
        for o in (-2, -1, 1, 2):
            hello(self.r, self.up(o))

        @pl.when(self.r != self.z)
        def _():
            hello(self.z, self.r)

        pl.semaphore_wait(barrier, 2 * (SIDE - 1) + FAR - 1 + 5 + jnp.where(self.r != self.z, 1, 0))

    def turn(self, src, dst, dst_local, sems):
        def away():
            return remote(src, dst, sems.at[0], sems.at[1], self.z, self.r)

        def here():
            return pltpu.make_async_copy(src, dst_local, sems.at[2])

        def start():
            @pl.when(self.r != self.z)
            def _():
                away().start()

            @pl.when(self.r == self.z)
            def _():
                here().start()

        def wait():
            @pl.when(self.r != self.z)
            def _():
                away().wait()

            @pl.when(self.r == self.z)
            def _():
                here().wait()

        return start, wait


def start_each(last, *copies):
    @pl.loop(1, last)
    def _(o):
        for copy in copies:
            copy(o).start()


def wait_each(last, *copies):
    @pl.loop(1, last)
    def _(o):
        for copy in copies:
            copy(o).wait()


SUB = 64
PACK = 16
GROUP = 4


def step(n, counts_ref, table_ref, ids_ref, slots_hbm, weights_hbm, cot_hbm, pooled_out, grad_out,
         fetched, piece_ref, slots_ref, weights_ref, cot_ref, hot, inc, slot_grad, table, table_wide, ids_x, ids_y, ids_in, grad_x, grad_y, grad_b, grad_in,
         pick, spread, tops, doubled, part, looked, rows_out, rows_b, rows_y, rows_x, near_a, near_b, near_c, near_d,
         total, far_out, far_in, piece,
         turn_sem, own_sem, far_sem, near_sem, id_sem, grad_sem, sum_sem, sum_far, row_sem, fin_sem, fetch_sem):
    seat = Seat(n)
    r, z, x, y, c, b = seat.r, seat.z, seat.x, seat.y, seat.c, seat.b
    bf16, f32 = jnp.bfloat16, jnp.float32
    bag, samples = slots_ref.shape
    capacity = hot.shape[1] * PACK
    width = cot_ref.shape[1]
    owners = inc.shape[0] // capacity
    middle, wide = FAR // 2, pick.shape[1]
    unit = piece.shape[0]
    low, high = pl.ds(0, capacity // 2), pl.ds(capacity // 2, capacity // 2)
    fetches = [pltpu.make_async_copy(src, dst, fetch_sem.at[k]) for k, (src, dst) in enumerate((
        (table_ref.at[pl.ds(pl.multiple_of(r * unit, unit), unit)], fetched),
        (slots_hbm, slots_ref),
        (weights_hbm, weights_ref),
        (cot_hbm, cot_ref),
    ))]
    for fetch in fetches:
        fetch.start()
    seat.greet()
    for fetch in fetches:
        fetch.wait()
    piece_ref[...] = fetched[...].astype(bf16)

    mine = table.at[place(z)]
    turn_start, turn_wait = seat.turn(piece_ref, table.at[place(r)], mine, turn_sem.at[0])
    turn_start()

    def far(o):
        return remote(mine, mine, far_sem.at[0, o], far_sem.at[1, o], r, seat.up(NEAR * o))

    def near(k, first, count, o):
        block = table.at[pl.ds(b * FAR + first, count)]
        return remote(block, block, near_sem.at[0, k], near_sem.at[1, k], r, seat.up(o))

    nears = [near(0, 0, FAR, 1), near(1, 0, FAR, -1), near(2, 0, middle, 2), near(3, middle, middle, -2)]

    def ship_ids(src, dst, k, to):
        return remote(src, dst, id_sem.at[0, k], id_sem.at[1, k], to, z)

    def x_ids(o):
        return ship_ids(ids_ref.at[seat.x_at(o)], ids_x.at[x], o, seat.along_x(o))

    def y_ids(o):
        return ship_ids(ids_x.at[:, seat.y_at(o)], ids_y.at[y], SIDE + o, seat.along_y(o))

    twin_ids = ship_ids(ids_y.at[:, :, 1 - c], ids_in.at[c], 0, seat.twin)

    def ship(src, dst, k, to):
        return remote(src, dst, grad_sem.at[0, k], grad_sem.at[1, k], to, z)

    def x_low(o):
        return ship(slot_grad.at[seat.x_at(o), :, :, low], grad_x.at[x], o, seat.along_x(o))

    def y_high(o):
        return ship(slot_grad.at[:, seat.y_at(o), :, high], grad_y.at[y], SIDE + o, seat.along_y(o))

    def y_low(o):
        return ship(grad_x.at[:, seat.y_at(o)], grad_b.at[y, :, :, low], 2 * SIDE + o, seat.along_y(o))

    def x_high(o):
        return ship(grad_y.at[:, seat.x_at(o)], grad_b.at[:, x, :, high], 3 * SIDE + o, seat.along_x(o))

    twin_grad = ship(grad_b.at[:, :, 1 - c], grad_in.at[c], 0, seat.twin)

    def ship_rows(src, dst, k, to):
        return remote(src, dst, row_sem.at[0, k], row_sem.at[1, k], to, z)

    def y_low_rows(o):
        return ship_rows(rows_b.at[:, seat.y_at(o), :, low], rows_y.at[y], o, seat.along_y(o))

    def x_high_rows(o):
        return ship_rows(rows_b.at[:, :, seat.x_at(o), high], rows_x.at[x], SIDE + o, seat.along_x(o))

    def x_low_rows(o):
        return ship_rows(rows_y.at[:, :, seat.x_at(o)], rows_out.at[x, :, :, low], 2 * SIDE + o, seat.along_x(o))

    def y_high_rows(o):
        return ship_rows(rows_x.at[:, :, seat.y_at(o)], rows_out.at[:, y, :, high], 3 * SIDE + o, seat.along_y(o))

    twin_rows = ship_rows(looked.at[1 - c], rows_b.at[c], 0, seat.twin)

    own = [pltpu.make_async_copy(src, dst, own_sem.at[k]) for k, (src, dst) in enumerate((
        (ids_ref.at[x], ids_x.at[x]),
        (ids_x.at[:, y], ids_y.at[y]),
        (ids_y.at[:, :, c], ids_in.at[c]),
        (slot_grad.at[x, :, :, low], grad_x.at[x]),
        (slot_grad.at[:, y, :, high], grad_y.at[y]),
        (grad_x.at[:, y], grad_b.at[y, :, :, low]),
        (grad_y.at[:, x], grad_b.at[:, x, :, high]),
        (grad_b.at[:, :, c], grad_in.at[c]),
        (looked.at[c], rows_b.at[c]),
        (rows_b.at[:, y, :, low], rows_y.at[y]),
        (rows_b.at[:, :, x, high], rows_x.at[x]),
        (rows_y.at[:, :, x], rows_out.at[x, :, :, low]),
        (rows_x.at[:, :, y], rows_out.at[:, y, :, high]),
    ))]

    def start_own(*which):
        for k in which:
            own[k].start()

    def wait_own(*which):
        for k in which:
            own[k].wait()

    def incidence(first, last):
        tiles = SUB // PACK

        @pl.loop(first, last)
        def _(owner):
            weights = jnp.where(slots_ref[...] // capacity == owner, weights_ref[...].astype(f32), 0.0)
            scales = [jnp.broadcast_to(weights[entry:entry + 1, :], (PACK, samples)).astype(bf16)[None]
                      for entry in range(bag)]

            def entries(at, lower, upper):
                if upper - lower == 1:
                    return hot[lower, at:at + tiles] * scales[lower]
                middle_entry = (lower + upper) // 2
                return entries(at, lower, middle_entry) + entries(at, middle_entry, upper)

            for at in range(0, capacity // PACK, tiles):
                slot = at * PACK + lax.broadcasted_iota(jnp.int32, (SUB, samples), 0)
                acc = entries(at, 0, bag).reshape(SUB, samples).astype(f32)
                acc = jnp.where(slot < counts_ref[owner], acc, 0.0)
                inc[pl.ds(pl.multiple_of(owner * capacity + at * PACK, SUB), SUB), :] = acc.astype(bf16)

    def slot_sums(first, last):
        @pl.loop(first, last)
        def _(k):
            size = GROUP * capacity
            block = inc[pl.ds(pl.multiple_of(k * size, size), size), :]
            sums = jnp.dot(block, cot_ref[...], preferred_element_type=f32).astype(bf16)
            half_side = SIDE // 2
            slot_grad[k // half_side, pl.ds(lax.rem(k, half_side) * half_side, half_side)] = sums.reshape(
                half_side, 2, capacity, width)

    def masks(first, last):
        one, zero = jnp.ones((capacity, 128), bf16), jnp.zeros((capacity, 128), bf16)
        lane = lax.broadcasted_iota(jnp.int32, (capacity, 128), 1).astype(f32).astype(bf16)
        row = lax.broadcasted_iota(jnp.int32, (128, capacity), 0).astype(f32).astype(bf16)

        def split(ids):
            lows = jnp.bitwise_and(ids, 127).astype(f32).astype(bf16)
            mids = jnp.bitwise_and(lax.shift_right_logical(ids, 7), wide // 128 - 1).astype(f32).astype(bf16)
            return lows, mids

        @pl.loop(first, last)
        def _(q):
            spot = ids_in[q // (SIDE * SIDE), lax.rem(q // SIDE, SIDE), lax.rem(q, SIDE)]
            spot = (lax.rem(spot // unit, NEAR) * FAR + spot // (unit * NEAR)) * unit + lax.rem(spot, unit)
            ids = jnp.broadcast_to(spot, (capacity, capacity))
            column = ids.astype(f32).T.astype(jnp.int32)
            here = pl.ds(pl.multiple_of(q * capacity, capacity), capacity)
            lows, mids = split(column)
            lit = jnp.where(lane == lows, one, zero)
            for tile in range(wide // 128):
                pick[here, tile * 128:(tile + 1) * 128] = jnp.where(mids == jnp.full_like(mids, tile), lit, zero)
            tops[here, :] = jnp.where(column >= wide, 1.0, 0.0)
            lows, mids = split(ids)
            lit = jnp.where(row == lows, one, zero)
            for tile in range(wide // 128):
                spread[tile * 128:(tile + 1) * 128, here] = jnp.where(mids == jnp.full_like(mids, tile), lit, zero)

    def sum_rows():
        @pl.loop(0, owners)
        def _(q):
            here = pl.ds(pl.multiple_of(q * capacity, capacity), capacity)
            cot = grad_in[q // (SIDE * SIDE), lax.rem(q // SIDE, SIDE), lax.rem(q, SIDE)].astype(f32)
            top = tops[here, :] > 0.5
            doubled[here, 0:width] = jnp.where(top, 0.0, cot).astype(bf16)
            doubled[here, width:2 * width] = jnp.where(top, cot, 0.0).astype(bf16)

        for k in range(NEAR // 2):
            size = FAR * unit
            sums = jnp.dot(spread[k * size:(k + 1) * size, :], doubled[...], preferred_element_type=f32)
            part[k] = sums[:, :width].reshape(FAR, unit, width)
            part[k + NEAR // 2] = sums[:, width:].reshape(FAR, unit, width)

    def look_up():
        table_wide[:, 0:width] = table[0:owners // 2].reshape(wide, width)
        table_wide[:, width:2 * width] = table[owners // 2:owners].reshape(wide, width)

        @pl.loop(0, owners // GROUP)
        def _(k):
            size = GROUP * capacity
            here = pl.ds(pl.multiple_of(k * size, size), size)
            both = jnp.dot(pick[here, :], table_wide[...], preferred_element_type=f32)
            rows = jnp.where(tops[here, :] > 0.5, both[:, width:], both[:, :width]).astype(bf16)
            looked[k // SIDE, lax.rem(k, SIDE)] = rows.reshape(SIDE, capacity, width)

    def pool():
        def add(k, acc):
            size = 2 * GROUP * capacity
            block = inc[pl.ds(pl.multiple_of(k * size, size), size), :]
            rows = rows_out[k].reshape(size, width)
            return acc + lax.dot_general(block, rows, (((0,), (0,)), ((), ())), preferred_element_type=f32)

        pooled = lax.fori_loop(0, SIDE, add, jnp.zeros((samples, width), f32))
        pooled_out[...] = pooled.astype(bf16)

    start_each(SIDE, x_ids)
    start_own(0)
    low_slot = lax.broadcasted_iota(jnp.int32, (capacity, samples), 0)
    for entry in range(bag):
        lit = jnp.where(low_slot == lax.rem(slots_ref[entry:entry + 1, :], capacity), 1.0, 0.0)
        hot[entry] = lit.astype(bf16).reshape(capacity // PACK, PACK, samples)
    incidence(0, owners // 2)
    turn_wait()
    start_each(FAR, far)
    wait_own(0)
    wait_each(SIDE, x_ids)
    start_each(SIDE, y_ids)
    start_own(1)
    incidence(owners // 2, owners)
    slot_sums(0, owners // GROUP)
    start_each(SIDE, x_low, y_high)
    start_own(3, 4)
    wait_own(1)
    wait_each(SIDE, y_ids)
    twin_ids.start()
    start_own(2)
    wait_own(2)
    twin_ids.wait()
    masks(0, owners // 2)
    wait_own(3, 4)
    wait_each(SIDE, x_low, y_high)
    start_each(SIDE, y_low, x_high)
    start_own(5, 6)
    wait_each(FAR, far)
    for copy in nears:
        copy.start()
    masks(owners // 2, owners)
    wait_own(5, 6)
    wait_each(SIDE, y_low, x_high)
    twin_grad.start()
    start_own(7)
    wait_own(7)
    twin_grad.wait()
    sum_rows()

    def sum_near(k, first, count, o, dst):
        block = part.at[lax.rem(b + o + NEAR, NEAR), pl.ds(first, count)]
        return remote(block, dst, sum_sem.at[0, k], sum_sem.at[1, k], r, seat.up(o))

    sum_nears = [sum_near(0, 0, FAR, 1, near_a), sum_near(1, 0, FAR, -1, near_b),
                 sum_near(2, 0, middle, 2, near_c), sum_near(3, middle, middle, -2, near_d)]

    def sum_far_copy(o):
        return remote(far_out.at[lax.rem(seat.a + o, FAR)], far_in.at[o], sum_far.at[0, o], sum_far.at[1, o],
                      r, seat.up(NEAR * o))

    for copy in sum_nears:
        copy.start()
    for copy in nears:
        copy.wait()
    look_up()
    twin_rows.start()
    start_own(8)
    wait_own(8)
    twin_rows.wait()
    start_each(SIDE, y_low_rows, x_high_rows)
    start_own(9, 10)
    for copy in sum_nears:
        copy.wait()
    for first, far_half in ((0, near_c), (middle, near_d)):
        here = pl.ds(first, middle)
        total[here] = (part[b, here] + near_a[here]) + (near_b[here] + far_half[...])
    far_out[...] = total[...].astype(bf16)
    start_each(FAR, sum_far_copy)
    wait_own(9, 10)
    wait_each(SIDE, y_low_rows, x_high_rows)
    start_each(SIDE, x_low_rows, y_high_rows)
    start_own(11, 12)
    wait_each(FAR, sum_far_copy)
    far_sum = total[seat.a]
    for o in range(1, FAR):
        far_sum = far_sum + far_in[o].astype(f32)
    piece[...] = far_sum

    upper, lower = pl.ds(0, unit // 2), pl.ds(unit // 2, unit // 2)

    def back(lines, k):
        afar = grad_out.at[z // (2 * SIDE), lax.rem(z // 2, SIDE), lax.rem(z, 2), lines]
        return seat.turn(piece.at[lines], afar, grad_out.at[x, y, c, lines], turn_sem.at[k])

    upper_start, upper_wait = back(upper, 1)
    lower_start, lower_wait = back(lower, 2)
    upper_start()
    lower_start()
    wait_own(11, 12)
    wait_each(SIDE, x_low_rows, y_high_rows)
    pool()

    def share(ref, k, to):
        return remote(ref, ref, fin_sem.at[0, k], fin_sem.at[1, k], to, z)

    def x_upper(o):
        return share(grad_out.at[x, y, c, upper], o, seat.along_x(o))

    def y_lower(o):
        return share(grad_out.at[x, y, c, lower], SIDE + o, seat.along_y(o))

    def y_upper(o):
        return share(grad_out.at[:, y, c, upper], 2 * SIDE + o, seat.along_y(o))

    def x_lower(o):
        return share(grad_out.at[x, :, c, lower], 3 * SIDE + o, seat.along_x(o))

    def twin_half(lines, k):
        return share(grad_out.at[:, :, c, lines], k, seat.twin)

    twins = twin_half(upper, 0), twin_half(lower, SIDE)
    upper_wait()
    start_each(SIDE, x_upper)
    lower_wait()
    start_each(SIDE, y_lower)
    wait_each(SIDE, x_upper)
    start_each(SIDE, y_upper)
    wait_each(SIDE, y_lower)
    start_each(SIDE, x_lower)
    wait_each(SIDE, y_upper)
    twins[0].start()
    wait_each(SIDE, x_lower)
    twins[1].start()
    twins[0].wait()
    twins[1].wait()


def per_device(n, table, accum, request_ids, send_counts, entry_slots, entry_weights, pooled_grad):
    rows, width = table.shape
    _, peers, capacity = request_ids.shape
    slots = peers * capacity
    samples, bag = entry_slots.shape
    unit = rows // n
    bf16, f32, i32 = jnp.bfloat16, jnp.float32, jnp.int32
    vmem = pl.BlockSpec(memory_space=pltpu.VMEM)
    hbm = pl.BlockSpec(memory_space=pltpu.HBM)
    dma = pltpu.SemaphoreType.DMA
    by_owner = (SIDE, SIDE, 2)
    by_core = (2, SIDE, SIDE)
    by_line = (SIDE, 2, SIDE)
    cut = capacity // 2

    pooled, grad = pl.pallas_call(
        functools.partial(step, n),
        in_specs=[pl.BlockSpec(memory_space=pltpu.SMEM), hbm, hbm, hbm, hbm, hbm],
        out_specs=[vmem, vmem],
        out_shape=[
            jax.ShapeDtypeStruct((samples, width), bf16),
            jax.ShapeDtypeStruct(by_owner + (unit, width), f32),
        ],
        scratch_shapes=[
            pltpu.VMEM((unit, width), f32),
            pltpu.VMEM((unit, width), bf16),
            pltpu.VMEM((bag, samples), i32),
            pltpu.VMEM((bag, samples), bf16),
            pltpu.VMEM((samples, width), bf16),
            pltpu.VMEM((bag, capacity // PACK, PACK, samples), bf16),
            pltpu.VMEM((slots, samples), bf16),
            pltpu.VMEM(by_owner + (capacity, width), bf16),
            pltpu.VMEM((n, unit, width), bf16),
            pltpu.VMEM((rows // 2, 2 * width), bf16),
            pltpu.VMEM(by_owner + (1, capacity), i32),
            pltpu.VMEM(by_owner + (1, capacity), i32),
            pltpu.VMEM(by_core + (1, capacity), i32),
            pltpu.VMEM(by_owner + (cut, width), bf16),
            pltpu.VMEM(by_owner + (cut, width), bf16),
            pltpu.VMEM(by_owner + (capacity, width), bf16),
            pltpu.VMEM(by_core + (capacity, width), bf16),
            pltpu.VMEM((slots, rows // 2), bf16),
            pltpu.VMEM((rows // 2, slots), bf16),
            pltpu.VMEM((slots, width), f32),
            pltpu.VMEM((slots, 2 * width), bf16),
            pltpu.VMEM((NEAR, FAR, unit, width), f32),
            pltpu.VMEM(by_core + (capacity, width), bf16),
            pltpu.VMEM(by_owner + (capacity, width), bf16),
            pltpu.VMEM(by_core + (capacity, width), bf16),
            pltpu.VMEM(by_line + (cut, width), bf16),
            pltpu.VMEM(by_line + (cut, width), bf16),
            pltpu.VMEM((FAR, unit, width), f32),
            pltpu.VMEM((FAR, unit, width), f32),
            pltpu.VMEM((FAR // 2, unit, width), f32),
            pltpu.VMEM((FAR // 2, unit, width), f32),
            pltpu.VMEM((FAR, unit, width), f32),
            pltpu.VMEM((FAR, unit, width), bf16),
            pltpu.VMEM((FAR, unit, width), bf16),
            pltpu.VMEM((unit, width), f32),
            dma((3, 3)), dma((13,)), dma((2, FAR)), dma((2, 4)), dma((2, 2 * SIDE)), dma((2, 4 * SIDE)),
            dma((2, 4)), dma((2, FAR)), dma((2, 4 * SIDE)), dma((2, 4 * SIDE)), dma((4,)),
        ],
        compiler_params=pltpu.CompilerParams(collective_id=0, has_side_effects=True, vmem_limit_bytes=63400000),
        name="step",
    )(send_counts.reshape(peers), table, request_ids.reshape(by_owner + (1, capacity)),
      entry_slots.T, entry_weights.T, pooled_grad)

    grad = grad.reshape(rows, width)
    fresh = accum + grad * grad
    return pooled, table - learn_rate * grad / jnp.sqrt(fresh), fresh


def solution(mesh):
    n = mesh.shape["mp"]
    both = ("replica", "mp")
    return jax.shard_map(
        functools.partial(per_device, n),
        mesh=mesh,
        in_specs=(
            P("mp", None),
            P("mp", None),
            P(both, None, None),
            P(both, None),
            P(both, None),
            P(both, None),
            P(both, None),
        ),
        out_specs=(P(both, None), P("mp", None), P("mp", None)),
        check_vma=False,
    )
```
